32 devices in a mesh: rows: 8 (over z, y), cols: 4 (over x, core).
Axes of the slice: x: 2, y: 2, z: 4, core: 2. Of those that a mesh axis runs over, the one named last changes fastest.
Arguments:
- features: bfloat16 [2048, 512], P(('rows', 'cols')), may hold values from -6 to 6
- w_query: bfloat16 [512, 512], replicated, may hold values from -0.25 to 0.25
- w_key: bfloat16 [512, 512], replicated, may hold values from -0.25 to 0.25
- w_value: bfloat16 [512, 512], replicated, may hold values from -0.25 to 0.25
- cotangent: bfloat16 [2048, 512], P(('rows', 'cols')), may hold values from -6 to 6
- block_pairs: int32 [8, 4, 6, 2], P('rows', 'cols'), may hold values from 0 to 3, as said below
- pair_count: int32 [8, 4], P('rows', 'cols'), may hold values from 1 to 6, as said below
- edge_mask: int32 [8, 4, 6, 128, 128], P('rows', 'cols'), may hold values 0 or 1
Outputs:
- attended: bfloat16 [2048, 512], P(('rows', 'cols'))
- input_grad: float32 [2048, 512], P(('rows', 'cols'))
The draws below stay inside these ranges and needn't reach their ends.
Inputs may be any that keep to these rules, and one draw needn't show every extreme that they name: `block_pairs`: each device's list holds distinct pairs; column 0 is a row block below 2, column 1 a column block below 4. `pair_count`: some device's count equals 6 in every draw.
All inputs are finite; a program needn't handle non-finite values. No bound on the sum of `edge_mask` on one device may be relied on, other than what follows from the above.
Results may differ from the reference program's by a relative error of at most 0.0068.
Values may be sent and summed in bfloat16 or wider, within the bound.
A program may use at most 128 MiB of HBM per device.

```python
import math
import jax
import jax.numpy as jnp
from jax import lax

HEADS = 8
HEAD_DIM = 64
D = 512
BLK = 128
CH = 64
REGIONS = 2048
RB = 2
CB = 4
MAXP = 6
N_ROWS = 8
N_COLS = 4


def draw_pair_count(key, part):
    first = jax.random.randint(jax.random.fold_in(key, 11), (N_ROWS, N_COLS), 1, MAXP + 1)
    second = jax.random.randint(jax.random.fold_in(key, 12), (N_ROWS, N_COLS), 1, MAXP + 1)
    counts = jnp.maximum(first * second // MAXP, 1).reshape(-1)
    heavy = jax.random.randint(jax.random.fold_in(key, 13), (), 0, N_ROWS * N_COLS)
    counts = jnp.where(jnp.arange(N_ROWS * N_COLS) == heavy, MAXP, counts)
    return counts.reshape(N_ROWS, N_COLS).astype(jnp.int32)


def draw_block_pairs(key, part):
    device_keys = jax.random.split(jax.random.fold_in(key, 21), N_ROWS * N_COLS)

    def one_list(device_key):
        order = jax.random.permutation(device_key, RB * CB)[:MAXP]
        return jnp.stack([order // CB, order % CB], axis=1)
    lists = jax.vmap(one_list)(device_keys)
    return lists.reshape(N_ROWS, N_COLS, MAXP, 2).astype(jnp.int32)


def place_ends(result, key, low, high):
    extent = result.shape
    spot = [jax.random.randint(jax.random.fold_in(key, axis), (), 0, extent[axis]) for axis in range(len(extent))]
    result = result.at[tuple(spot)].set(low)
    longest = extent.index(max(extent))
    spot[longest] = (spot[longest] + 1) % extent[longest]
    return result.at[tuple(spot)].set(high)


def levels(key, dims, cuts, low, largest):
    gain = 1.0
    for position, parts in cuts:
        draws = jax.random.uniform(jax.random.fold_in(jax.random.fold_in(key, 6), position), (parts,), jnp.float32, low / len(cuts), largest / len(cuts))
        gain = gain * jnp.repeat(jnp.exp(draws), dims[position] // parts).reshape((-1,) + (1,) * (len(dims) - 1 - position))
    return gain


def centred(own_key, extent, scale, reach, cuts=(), dtype=jnp.bfloat16):
    array = scale * jax.random.normal(own_key, extent, jnp.float32)
    if cuts:
        array = array * levels(own_key, extent, cuts, -0.22, 0.18)
    return jnp.clip(array, -reach, reach).astype(dtype)


def setup_inputs(seed: int = 0) -> dict:
    keys = jax.random.split(jax.random.key(seed), 9)
    return {
        "features": centred(keys[0], (REGIONS, D), 1.0, 6.0, ((0, 32),)),
        "w_query": centred(keys[1], (D, D), D ** -0.5, 0.25),
        "w_key": centred(keys[2], (D, D), D ** -0.5, 0.25),
        "w_value": centred(keys[3], (D, D), D ** -0.5, 0.25),
        "cotangent": centred(keys[4], (REGIONS, D), 1.0, 6.0, ((0, 32),)),
        "block_pairs": draw_block_pairs(jax.random.fold_in(keys[8], 71), 0),
        "pair_count": draw_pair_count(jax.random.fold_in(keys[8], 71), 0),
        "edge_mask": place_ends((jax.random.randint(keys[7], (N_ROWS, N_COLS, MAXP, BLK, BLK), 0, 4) < 1).astype(jnp.int32), jax.random.fold_in(keys[7], 1), 0, 1),
    }


SCORE_BOUND = 4.0

def project(features, weight):
    return jnp.dot(features, weight, preferred_element_type=jnp.float32).astype(jnp.bfloat16)

def rounded(values):
    return lax.optimization_barrier(values.astype(jnp.bfloat16)).astype(jnp.float32)

def split_heads(table):
    return table.astype(jnp.float32).reshape(table.shape[0], HEADS, HEAD_DIM)

def edge_terms(query_rows, key_rows, mask_rows):
    score = jnp.einsum('ihd,jhd->hij', split_heads(query_rows), split_heads(key_rows))
    bounded = jnp.tanh(score * (1.0 / (math.sqrt(HEAD_DIM) * SCORE_BOUND)))
    weight = mask_rows.astype(jnp.float32)[None] * jnp.exp(SCORE_BOUND * bounded)
    return (weight, bounded)

def self_terms(query, keyed):
    score = lax.optimization_barrier(jnp.sum(split_heads(query) * split_heads(keyed), axis=2))
    bounded = jnp.tanh(score * (1.0 / (math.sqrt(HEAD_DIM) * SCORE_BOUND)))
    return (jnp.exp(SCORE_BOUND * bounded), bounded)

def column_range(table, column):
    grouped = table.reshape(N_ROWS, N_COLS, CH, D)
    picked = lax.dynamic_index_in_dim(grouped, column, 1, keepdims=False)
    return picked.reshape(N_ROWS * CH, D)

def add_rows(table, addend, first_row):
    current = lax.dynamic_slice_in_dim(table, first_row, addend.shape[0], 0)
    return lax.dynamic_update_slice_in_dim(table, current + addend, first_row, 0)

def high_dot(grads, weight):
    return jnp.dot(grads, weight.astype(jnp.float32).T, precision=lax.Precision.HIGHEST)

def reference(features, w_query, w_key, w_value, cotangent, block_pairs, pair_count, edge_mask):
    query = project(features, w_query)
    keyed = project(features, w_key)
    valued = project(features, w_value)
    part_rows = CH * N_COLS
    range_rows = CH * N_ROWS
    device_total = N_ROWS * N_COLS
    pair_lists = block_pairs.reshape(device_total, MAXP, 2)
    mask_lists = edge_mask.reshape(device_total, MAXP, BLK, BLK)
    totals = pair_count.reshape(device_total)
    inverse_root = 1.0 / math.sqrt(HEAD_DIM)

    def device_inputs(device):
        row_part = device // N_COLS
        column = device % N_COLS
        return (row_part, column, pair_lists[device], mask_lists[device], totals[device])

    def forward_device(device, sums):
        row_part, column, pair_list, mask_list, pair_total = device_inputs(device)
        key_cols = column_range(keyed, column)
        value_cols = column_range(valued, column)

        def forward_pair(slot, inner):
            numerator, denominator = inner
            first_row = (row_part * part_rows + pair_list[slot, 0] * BLK).astype(jnp.int32)
            first_col = (pair_list[slot, 1] * BLK).astype(jnp.int32)
            query_rows = lax.dynamic_slice_in_dim(query, first_row, BLK, 0)
            key_rows = lax.dynamic_slice_in_dim(key_cols, first_col, BLK, 0)
            value_rows = lax.dynamic_slice_in_dim(value_cols, first_col, BLK, 0)
            weight, bounded = edge_terms(query_rows, key_rows, mask_list[slot])
            numerator_part = jnp.einsum('hij,jhd->ihd', rounded(weight), split_heads(value_rows)).reshape(BLK, D)
            numerator = add_rows(numerator, numerator_part, first_row)
            denominator = add_rows(denominator, lax.optimization_barrier(jnp.sum(weight, axis=2)).T, first_row)
            return (numerator, denominator)
        return lax.fori_loop(jnp.int32(0), pair_total, forward_pair, sums)
    start_sums = (jnp.zeros((REGIONS, D), jnp.float32), jnp.zeros((REGIONS, HEADS), jnp.float32))
    numerator, denominator = lax.fori_loop(jnp.int32(0), jnp.int32(device_total), forward_device, start_sums)
    self_weight, self_bound = self_terms(query, keyed)
    numerator = numerator + (rounded(self_weight)[:, :, None] * split_heads(valued)).reshape(REGIONS, D)
    denominator = denominator + self_weight
    inverse = 1.0 / denominator
    out_heads = numerator.reshape(REGIONS, HEADS, HEAD_DIM) * inverse[:, :, None]
    attended = out_heads.reshape(REGIONS, D).astype(jnp.bfloat16)
    grad_heads = split_heads(cotangent)
    delta = lax.optimization_barrier(jnp.sum(grad_heads * out_heads, axis=2))

    def backward_device(device, sums):
        row_part, column, pair_list, mask_list, pair_total = device_inputs(device)
        key_cols = column_range(keyed, column)
        value_cols = column_range(valued, column)

        def backward_pair(slot, inner):
            query_grad, range_grad = inner
            first_row = (row_part * part_rows + pair_list[slot, 0] * BLK).astype(jnp.int32)
            first_col = (pair_list[slot, 1] * BLK).astype(jnp.int32)
            query_rows = lax.dynamic_slice_in_dim(query, first_row, BLK, 0)
            grad_rows = lax.dynamic_slice_in_dim(cotangent, first_row, BLK, 0)
            key_rows = lax.dynamic_slice_in_dim(key_cols, first_col, BLK, 0)
            value_rows = lax.dynamic_slice_in_dim(value_cols, first_col, BLK, 0)
            weight, bounded = edge_terms(query_rows, key_rows, mask_list[slot])
            grad_value = jnp.einsum('ihd,jhd->hij', split_heads(grad_rows), split_heads(value_rows))
            inverse_rows = lax.dynamic_slice_in_dim(inverse, first_row, BLK, 0).T[:, :, None]
            delta_rows = lax.dynamic_slice_in_dim(delta, first_row, BLK, 0).T[:, :, None]
            scaled = weight * inverse_rows
            grad_score = rounded(scaled * (grad_value - delta_rows) * (1.0 - bounded * bounded) * inverse_root)
            value_share = rounded(scaled)
            query_part = jnp.einsum('hij,jhd->ihd', grad_score, split_heads(key_rows)).reshape(BLK, D)
            key_part = jnp.einsum('hij,ihd->jhd', grad_score, split_heads(query_rows)).reshape(BLK, D)
            value_part = jnp.einsum('hij,ihd->jhd', value_share, split_heads(grad_rows)).reshape(BLK, D)
            query_grad = add_rows(query_grad, query_part, first_row)
            range_first = (column * range_rows + first_col).astype(jnp.int32)
            range_grad = add_rows(range_grad, jnp.concatenate([key_part, value_part], axis=1), range_first)
            return (query_grad, range_grad)
        return lax.fori_loop(jnp.int32(0), pair_total, backward_pair, sums)
    start_grads = (jnp.zeros((REGIONS, D), jnp.float32), jnp.zeros((N_COLS * range_rows, 2 * D), jnp.float32))
    query_grad, range_grad = lax.fori_loop(jnp.int32(0), jnp.int32(device_total), backward_device, start_grads)
    key_value = range_grad.reshape(N_COLS, N_ROWS, CH, 2 * D).transpose(1, 0, 2, 3).reshape(REGIONS, 2 * D)
    self_scaled = self_weight * inverse
    self_value_dot = lax.optimization_barrier(jnp.sum(grad_heads * split_heads(valued), axis=2))
    self_grad = rounded(self_scaled * (self_value_dot - delta) * (1.0 - self_bound * self_bound) * inverse_root)
    self_share = rounded(self_scaled)
    query_grad = query_grad + (self_grad[:, :, None] * split_heads(keyed)).reshape(REGIONS, D)
    key_grad = key_value[:, :D] + (self_grad[:, :, None] * split_heads(query)).reshape(REGIONS, D)
    value_grad = key_value[:, D:] + (self_share[:, :, None] * grad_heads).reshape(REGIONS, D)
    input_grad = high_dot(query_grad, w_query) + high_dot(key_grad, w_key) + high_dot(value_grad, w_value)
    return (attended, input_grad)
```

```python
import functools
import math

import jax
import jax.numpy as jnp
from jax import lax
from jax.experimental import pallas as pl
from jax.experimental.pallas import tpu as pltpu
from jax.sharding import PartitionSpec as P

HEADS = 8
SCORE_BOUND = 4.0
LANES = 128
MESH = pl.DeviceIdType.MESH
F32 = jnp.float32
BF16 = jnp.bfloat16


def dot(a, b):
    return jnp.dot(a, b, preferred_element_type=F32)


def dot_t(a, b):
    return lax.dot_general(a, b, (((1,), (1,)), ((), ())), preferred_element_type=F32)


def kernel(
    row_total, col_total, keep,
    feat, wq, wk, wv, cot, pairs, count, mask,
    att_out, grad_out,
    fcol, frow, crow, k_s, v_s, kt_s, vt_s, q_s, qtm, ctm, mask_t, e_s, t_s,
    num_t, den_s, inv_s, dl_s, qg_t, kg_s, vg_s,
    stat_send, stat_recv, num_send, num_recv, qg_send, qg_recv, rg_send, rg_recv,
    col_ss, col_rs, fr_ss, fr_rs, cr_ss, cr_rs, st_ss, st_rs, nu_ss, nu_rs,
    qg_ss, qg_rs, rg_ss, rg_rs,
):
    owned, width = feat.shape
    slots, block, _ = mask.shape
    head = width // HEADS
    part = owned * col_total
    row_blocks = part // block
    chunks = owned * row_total // block
    per = block // owned
    me_r = lax.axis_index("rows")
    me_c = lax.axis_index("cols")
    scale = 1.0 / (math.sqrt(head) * SCORE_BOUND)
    inverse_root = 1.0 / math.sqrt(head)

    def remote(src, dst, ss, rs, axis, peer):
        return pltpu.make_async_remote_copy(
            src_ref=src, dst_ref=dst, send_sem=ss, recv_sem=rs,
            device_id={axis: peer}, device_id_type=MESH,
        )

    def arrived(buf, ss, rs, axis, src):
        remote(buf.at[src], buf.at[src], ss.at[src], rs.at[src], axis, src).wait_recv()

    row_peers = [lax.rem(me_r + d, row_total) for d in range(1, row_total)]
    col_peers = [lax.rem(me_c + d, col_total) for d in range(1, col_total)]

    barrier = pltpu.get_barrier_semaphore()
    for peer in row_peers:
        pl.semaphore_signal(barrier, inc=1, device_id={"rows": peer}, device_id_type=MESH)
    for peer in col_peers:
        pl.semaphore_signal(barrier, inc=1, device_id={"cols": peer}, device_id_type=MESH)
    pl.semaphore_wait(barrier, row_total + col_total - 2)

    for peer in col_peers:
        remote(feat, frow.at[me_c], fr_ss.at[peer], fr_rs.at[me_c], "cols", peer).start()
    for peer in row_peers:
        remote(feat, fcol.at[me_r], col_ss.at[peer], col_rs.at[me_r], "rows", peer).start()
    for peer in col_peers:
        remote(cot, crow.at[me_c], cr_ss.at[peer], cr_rs.at[me_c], "cols", peer).start()

    fcol[me_r] = feat[...]
    frow[me_c] = feat[...]
    crow[me_c] = cot[...]
    num_t[...] = jnp.zeros_like(num_t)
    den_s[...] = jnp.zeros_like(den_s)
    qg_t[...] = jnp.zeros_like(qg_t)

    live_total = count[0]

    def mask_chunk(k, carry):
        for b in range(row_blocks):
            def find(s, found):
                hit = (pairs[2 * s] == b) & (pairs[2 * s + 1] == k) & (s < live_total)
                return jnp.where(hit, s, found)

            found = lax.fori_loop(0, slots, find, jnp.int32(-1), unroll=slots <= 8)
            live = (found >= 0).astype(F32)
            tile = mask[jnp.maximum(found, 0)].astype(F32) * live
            j = lax.broadcasted_iota(jnp.int32, (block, block), 0) + k * block
            i = lax.broadcasted_iota(jnp.int32, (block, block), 1) + b * block
            own = i - me_c * owned
            same = (own == j - me_r * owned) & (own >= 0) & (own < owned)
            first = pl.multiple_of(k * block, block)
            mask_t[pl.ds(first, block), b * block:(b + 1) * block] = tile.T + same.astype(F32)
        return carry

    lax.fori_loop(0, chunks, mask_chunk, 0)

    for peer in col_peers:
        arrived(frow, fr_ss, fr_rs, "cols", peer)
    query = dot(frow[...].reshape(part, width), wq[...])
    q_s[...] = query.astype(BF16)
    query_t = query.T.astype(BF16)
    for h in range(HEADS):
        low, high = (h % 2) * head, (h % 2 + 1) * head
        other = head - low
        qtm[h, low:high, :] = query_t[h * head:(h + 1) * head, :]
        qtm[h, other:other + head, :] = jnp.zeros((head, part), BF16)

    own_chunk = me_r // per

    def terms(h, kp, m):
        t = jnp.tanh(dot(kp, qtm[h]) * scale)
        return m * jnp.exp(SCORE_BOUND * t), t

    def forward(step, carry):
        k = lax.rem(own_chunk + step, chunks)
        first = pl.multiple_of(k * block, block)
        for o in range(per):
            src = k * per + o

            @pl.when(src != me_r)
            def _():
                arrived(fcol, col_ss, col_rs, "rows", src)
        rows = fcol[pl.ds(k * per, per)].reshape(block, width)
        keyed = dot(rows, wk[...])
        k_s[pl.ds(first, block), :] = keyed.astype(BF16)
        kt_s[k] = keyed.T.astype(BF16)
        valued = dot(rows, wv[...])
        v_s[pl.ds(first, block), :] = valued.astype(BF16)
        vt_s[k] = valued.T.astype(BF16)

        def pair(p, inner):
            kp = k_s[pl.ds(first, block), pl.ds(pl.multiple_of(p * LANES, LANES), LANES)]
            m = mask_t[pl.ds(first, block), :]
            for a in range(2):
                h = 2 * p + a
                e, t = terms(h, kp, m)
                if keep:
                    e_s[h, pl.ds(first, block), :] = e
                    t_s[h, pl.ds(first, block), :] = t
                vt = vt_s[k, pl.ds(pl.multiple_of(h * head, head), head), :]
                num_t[h] += dot(vt, e.astype(BF16))
                den_s[h] += jnp.sum(e.reshape(block // 8, 8, part), axis=0)
            return inner

        lax.fori_loop(0, HEADS // 2, pair, 0)
        return carry

    lax.fori_loop(0, chunks, forward, 0)

    for peer in col_peers:
        arrived(crow, cr_ss, cr_rs, "cols", peer)
    grad_t = crow[...].reshape(part, width).astype(F32).T
    for h in range(HEADS):
        low, high = (h % 2) * head, (h % 2 + 1) * head
        other = head - low
        ctm[h, low:high, :] = grad_t[h * head:(h + 1) * head, :].astype(BF16)
        ctm[h, other:other + head, :] = jnp.zeros((head, part), BF16)

    stat_send[0] = jnp.sum(den_s[...], axis=1)
    stat_send[1] = jnp.sum(num_t[...] * grad_t.reshape(HEADS, head, part), axis=1)
    for peer in col_peers:
        remote(stat_send, stat_recv.at[me_c], st_ss.at[peer], st_rs.at[me_c], "cols", peer).start()
    stat_recv[me_c] = stat_send[...]
    for peer in col_peers:
        arrived(stat_recv, st_ss, st_rs, "cols", peer)
    total = jnp.sum(stat_recv[...], axis=0)
    inverse = 1.0 / total[0]
    inv_s[...] = inverse
    dl_s[...] = total[1] * inverse

    out_part = (num_t[...] * inverse[:, None, :]).reshape(width, part).T
    num_send[...] = out_part.astype(BF16).reshape(col_total, owned, width)
    for peer in col_peers:
        remote(num_send.at[peer], num_recv.at[me_c], nu_ss.at[peer], nu_rs.at[me_c], "cols", peer).start()
    num_recv[me_c] = num_send[me_c]

    lane = lax.broadcasted_iota(jnp.int32, (part, LANES), 1)

    def backward(step, carry):
        k = lax.rem(own_chunk + step + 1, chunks)
        first = pl.multiple_of(k * block, block)

        def pair(p, inner):
            lanes = pl.ds(pl.multiple_of(p * LANES, LANES), LANES)
            vp = v_s[pl.ds(first, block), lanes]
            qp = q_s[:, lanes]
            cp = crow[:, :, lanes].reshape(part, LANES)
            kg = jnp.zeros((block, LANES), F32)
            vg = jnp.zeros((block, LANES), F32)
            for a in range(2):
                h = 2 * p + a
                if keep:
                    e, t = e_s[h, pl.ds(first, block), :], t_s[h, pl.ds(first, block), :]
                else:
                    e, t = terms(h, k_s[pl.ds(first, block), lanes], mask_t[pl.ds(first, block), :])
                share = e * inv_s[pl.ds(h, 1), :]
                grad_value = dot(vp, ctm[h])
                g = share * (grad_value - dl_s[pl.ds(h, 1), :]) * ((1.0 - t * t) * inverse_root)
                gb, sb = g.astype(BF16), share.astype(BF16)
                mine = (lane >= a * head) & (lane < (a + 1) * head)
                kt = kt_s[k, pl.ds(pl.multiple_of(h * head, head), head), :]
                qg_t[h] += dot(kt, gb)
                kg += dot(gb, jnp.where(mine, qp, jnp.zeros_like(qp)))
                vg += dot(sb, jnp.where(mine, cp, jnp.zeros_like(cp)))
            kg_s[:, lanes] = kg.astype(BF16)
            vg_s[:, lanes] = vg.astype(BF16)
            return inner

        lax.fori_loop(0, HEADS // 2, pair, 0)
        sums = dot_t(kg_s[...], wk[...]) + dot_t(vg_s[...], wv[...])
        rg_send[pl.ds(k * per, per)] = sums.astype(BF16).reshape(per, owned, width)
        for o in range(per):
            dst = k * per + o

            @pl.when(dst != me_r)
            def _():
                remote(
                    rg_send.at[dst], rg_recv.at[me_r], rg_ss.at[dst], rg_rs.at[me_r], "rows", dst
                ).start()
        return carry

    lax.fori_loop(0, chunks, backward, 0)
    rg_recv[me_r] = rg_send[me_r]

    query_grad = qg_t[...].reshape(width, part).T.astype(BF16)
    qg_send[...] = dot_t(query_grad, wq[...]).astype(BF16).reshape(col_total, owned, width)
    for peer in col_peers:
        remote(qg_send.at[peer], qg_recv.at[me_c], qg_ss.at[peer], qg_rs.at[me_c], "cols", peer).start()
    qg_recv[me_c] = qg_send[me_c]

    for peer in col_peers:
        arrived(num_recv, nu_ss, nu_rs, "cols", peer)
    att_out[...] = jnp.sum(num_recv[...].astype(F32), axis=0).astype(BF16)
    for peer in col_peers:
        arrived(qg_recv, qg_ss, qg_rs, "cols", peer)
    for peer in row_peers:
        arrived(rg_recv, rg_ss, rg_rs, "rows", peer)
    grad_out[...] = jnp.sum(qg_recv[...].astype(F32), axis=0) + jnp.sum(
        rg_recv[...].astype(F32), axis=0
    )

    for peer in col_peers:
        remote(feat, frow.at[me_c], fr_ss.at[peer], fr_rs.at[me_c], "cols", peer).wait_send()
        remote(cot, crow.at[me_c], cr_ss.at[peer], cr_rs.at[me_c], "cols", peer).wait_send()
        remote(stat_send, stat_recv.at[me_c], st_ss.at[peer], st_rs.at[me_c], "cols", peer).wait_send()
        remote(num_send.at[peer], num_recv.at[me_c], nu_ss.at[peer], nu_rs.at[me_c], "cols", peer).wait_send()
        remote(qg_send.at[peer], qg_recv.at[me_c], qg_ss.at[peer], qg_rs.at[me_c], "cols", peer).wait_send()
    for peer in row_peers:
        remote(feat, fcol.at[me_r], col_ss.at[peer], col_rs.at[me_r], "rows", peer).wait_send()
        remote(rg_send.at[peer], rg_recv.at[me_r], rg_ss.at[peer], rg_rs.at[me_r], "rows", peer).wait_send()


def local(row_total, col_total, features, w_query, w_key, w_value, cotangent, block_pairs, pair_count, edge_mask):
    owned, width = features.shape
    slots, block = edge_mask.shape[2], edge_mask.shape[3]
    part = owned * col_total
    span = owned * row_total
    chunks = span // block
    head = width // HEADS
    keep = span <= 512
    kept = (HEADS, span, part) if keep else (1, 8, LANES)
    vmem = pl.BlockSpec(memory_space=pltpu.VMEM)
    smem = pl.BlockSpec(memory_space=pltpu.SMEM)

    def buf(*shape, dtype=BF16):
        return pltpu.VMEM(shape, dtype)

    by_col = buf(col_total, owned, width)
    by_row = buf(row_total, owned, width)
    col_sem = pltpu.SemaphoreType.DMA((col_total,))
    row_sem = pltpu.SemaphoreType.DMA((row_total,))
    scratch = [
        by_row, by_col, by_col,
        buf(span, width), buf(span, width),
        buf(chunks, width, block), buf(chunks, width, block),
        buf(part, width), buf(HEADS, LANES, part), buf(HEADS, LANES, part),
        buf(span, part, dtype=F32), buf(*kept, dtype=F32), buf(*kept, dtype=F32),
        buf(HEADS, head, part, dtype=F32), buf(HEADS, 8, part, dtype=F32),
        buf(HEADS, part, dtype=F32), buf(HEADS, part, dtype=F32),
        buf(HEADS, head, part, dtype=F32), buf(block, width), buf(block, width),
        buf(2, HEADS, part, dtype=F32), buf(col_total, 2, HEADS, part, dtype=F32),
        by_col, by_col, by_col, by_col, by_row, by_row,
        row_sem, row_sem, col_sem, col_sem, col_sem, col_sem, col_sem, col_sem, col_sem, col_sem,
        col_sem, col_sem, row_sem, row_sem,
    ]
    return pl.pallas_call(
        functools.partial(kernel, row_total, col_total, keep),
        out_shape=(
            jax.ShapeDtypeStruct((owned, width), BF16),
            jax.ShapeDtypeStruct((owned, width), F32),
        ),
        in_specs=[vmem, vmem, vmem, vmem, vmem, smem, smem, vmem],
        out_specs=(vmem, vmem),
        scratch_shapes=scratch,
        compiler_params=pltpu.CompilerParams(
            collective_id=0, has_side_effects=True, vmem_limit_bytes=56 * 1024 * 1024
        ),
    )(
        features, w_query, w_key, w_value, cotangent,
        block_pairs.reshape(-1), pair_count.reshape(-1), edge_mask.reshape(slots, block, block),
    )


def solution(mesh):
    in_specs = (
        P(("rows", "cols"), None),
        P(),
        P(),
        P(),
        P(("rows", "cols"), None),
        P("rows", "cols", None, None),
        P("rows", "cols"),
        P("rows", "cols", None, None, None),
    )
    out_specs = (P(("rows", "cols"), None), P(("rows", "cols"), None))
    body = functools.partial(local, mesh.shape["rows"], mesh.shape["cols"])
    return jax.shard_map(body, mesh=mesh, in_specs=in_specs, out_specs=out_specs, check_vma=False)
```

```python
import functools
import math

import jax
import jax.numpy as jnp
from jax import lax
from jax.experimental import pallas as pl
from jax.experimental.pallas import tpu as pltpu
from jax.sharding import PartitionSpec as P

HEADS = 8
SCORE_BOUND = 4.0
LANES = 128
MESH = pl.DeviceIdType.MESH
F32 = jnp.float32
BF16 = jnp.bfloat16


def dot(a, b):
    return jnp.dot(a, b, preferred_element_type=F32)


def dot_t(a, b):
    return lax.dot_general(a, b, (((1,), (1,)), ((), ())), preferred_element_type=F32)


def kernel(
    row_total, col_total, keep,
    feat, wq_in, wk_in, wv_in, cot, pairs, count, mask_in,
    att_out, grad_out,
    wq, wk, wv, mask, fcol, frow, crow, k_s, v_s, kt_s, vt_s, q_s, qtm, ctm, mask_t, e_s, a_s, b_s,
    num_t, den_s, inv_s, dl_s, qg_t, kg_s, vg_s,
    stat_send, stat_recv, num_send, num_recv, qg_send, qg_recv,
    tw_send, tw_recv, rg_own, rg_send, rg_recv,
    load_s, col_ss, col_fs, col_rs, fr_ss, fr_rs, cr_ss, cr_rs, st_ss, st_rs, nu_ss, nu_rs,
    qg_ss, qg_rs, tw_ss, tw_rs, rg_ss, rg_rs,
):
    owned, width = feat.shape
    slots, block, _ = mask.shape
    head = width // HEADS
    part = owned * col_total
    row_blocks = part // block
    chunks = owned * row_total // block
    per = block // owned
    me_r = lax.axis_index("rows")
    me_c = lax.axis_index("cols")
    scale = 1.0 / (math.sqrt(head) * SCORE_BOUND)
    inverse_root = 1.0 / math.sqrt(head)

    def flip(index, amount, count_all):
        if count_all & (count_all - 1):
            return lax.rem(index + amount, count_all)
        out, bit = 0, 1
        while bit < count_all:
            out = out + bit * lax.rem(lax.div(index, bit) + lax.div(jnp.int32(amount), bit), 2)
            bit *= 2
        return out

    me_k, side = lax.div(me_r, per), lax.rem(me_r, per)
    twin_r = me_k * per + (1 - side)
    line = [flip(me_k, d, chunks) for d in range(1, chunks)]
    half, side_c = lax.div(me_c, 2), lax.rem(me_c, 2)
    twin_c = half * 2 + (1 - side_c)
    halves = [lax.rem(half + d, col_total // 2) for d in range(1, col_total // 2)]
    col_line = [x * 2 + side_c for x in halves]
    col_cross = [x * 2 + (1 - side_c) for x in halves]
    col_peers = col_cross + col_line + [twin_c]

    def remote(src, dst, ss, rs, axis, peer):
        return pltpu.make_async_remote_copy(
            src_ref=src, dst_ref=dst, send_sem=ss, recv_sem=rs,
            device_id={axis: peer}, device_id_type=MESH,
        )

    def arrived(buf, ss, rs, axis, src):
        remote(buf.at[src], buf.at[src], ss.at[src], rs.at[src], axis, src).wait_recv()

    loads = [
        pltpu.make_async_copy(src, dst, load_s.at[n])
        for n, (src, dst) in enumerate(
            [
                (mask_in, mask), (feat, frow.at[me_c]), (feat, fcol.at[me_r]), (cot, crow.at[me_c]),
                (wq_in, wq), (wk_in, wk), (wv_in, wv),
            ]
        )
    ]

    barrier = pltpu.get_barrier_semaphore()
    for peer in [twin_r] + [x * per + side for x in line]:
        pl.semaphore_signal(barrier, inc=1, device_id={"rows": peer}, device_id_type=MESH)
    for peer in col_peers:
        pl.semaphore_signal(barrier, inc=1, device_id={"cols": peer}, device_id_type=MESH)
    for load in loads:
        load.start()
    pl.semaphore_wait(barrier, chunks + col_total - 1)

    sends = []

    def send(*args):
        copy = remote(*args)
        copy.start()
        sends.append(copy)

    for peer in col_line:
        send(feat, frow.at[me_c], fr_ss.at[peer], fr_rs.at[me_c], "cols", peer)
    send(feat, fcol.at[me_r], col_fs.at[me_k], col_rs.at[me_r], "rows", twin_r)
    for x in line:
        send(feat, fcol.at[me_r], col_ss.at[x], col_rs.at[me_r], "rows", x * per + side)
    send(feat, frow.at[me_c], fr_ss.at[me_c], fr_rs.at[me_c], "cols", twin_c)
    for peer in col_line:
        send(cot, crow.at[me_c], cr_ss.at[peer], cr_rs.at[me_c], "cols", peer)
    send(cot, crow.at[me_c], cr_ss.at[me_c], cr_rs.at[me_c], "cols", twin_c)

    num_t[...] = jnp.zeros_like(num_t)
    den_s[...] = jnp.zeros_like(den_s)
    qg_t[...] = jnp.zeros_like(qg_t)
    for h in range(HEADS):
        other = (1 - h % 2) * head
        qtm[h, other:other + head, :] = jnp.zeros((head, part), BF16)
        ctm[h, other:other + head, :] = jnp.zeros((head, part), BF16)

    live_total = count[0, 0]
    loads[0].wait()

    def mask_chunk(k, carry):
        for b in range(row_blocks):
            def find(s, found):
                hit = (pairs[s, 0] == b) & (pairs[s, 1] == k) & (s < live_total)
                return jnp.where(hit, s, found)

            found = lax.fori_loop(0, slots, find, jnp.int32(-1), unroll=slots <= 8)
            live = (found >= 0).astype(F32)
            tile = mask[jnp.maximum(found, 0)].astype(F32) * live
            j = lax.broadcasted_iota(jnp.int32, (block, block), 0) + k * block
            i = lax.broadcasted_iota(jnp.int32, (block, block), 1) + b * block
            own = i - me_c * owned
            same = (own == j - me_r * owned) & (own >= 0) & (own < owned)
            first = pl.multiple_of(k * block, block)
            mask_t[pl.ds(first, block), b * block:(b + 1) * block] = tile.T + same.astype(F32)
        return carry

    lax.fori_loop(0, chunks, mask_chunk, 0)

    def share_columns(buf, ss, rs):
        for peer in col_line:
            arrived(buf, ss, rs, "cols", peer)
            send(buf.at[peer], buf.at[peer], ss.at[peer + 1 - 2 * side_c], rs.at[peer], "cols", twin_c)
        for peer in [twin_c] + col_cross:
            arrived(buf, ss, rs, "cols", peer)

    for load in loads[1:5]:
        load.wait()
    share_columns(frow, fr_ss, fr_rs)
    query = dot(frow[...].reshape(part, width), wq[...])
    q_s[...] = query.astype(BF16)
    query_t = query.T.astype(BF16)
    for h in range(HEADS):
        low, high = (h % 2) * head, (h % 2 + 1) * head
        qtm[h, low:high, :] = query_t[h * head:(h + 1) * head, :]
    share_columns(crow, cr_ss, cr_rs)
    grad_t = crow[...].reshape(part, width).astype(F32).T.astype(BF16)
    for h in range(HEADS):
        low, high = (h % 2) * head, (h % 2 + 1) * head
        ctm[h, low:high, :] = grad_t[h * head:(h + 1) * head, :]
    for load in loads[5:]:
        load.wait()

    def terms(h, kp, vp, m):
        t = jnp.tanh(dot(kp, qtm[h]) * scale)
        e = m * jnp.exp(SCORE_BOUND * t)
        slope = e * ((1.0 - t * t) * inverse_root)
        return e, slope * dot(vp, ctm[h]), slope

    def weights_only(h, kp, m):
        return m * jnp.exp(SCORE_BOUND * jnp.tanh(dot(kp, qtm[h]) * scale))

    def forward(step, carry):
        k = flip(me_k, step, chunks)
        first = pl.multiple_of(k * block, block)

        @pl.when(step + 1 < chunks)
        def _():
            nxt = flip(me_k, step + 1, chunks)
            slot = nxt * per + side
            arrived(fcol, col_rs, col_rs, "rows", slot)
            remote(fcol.at[slot], fcol.at[slot], col_fs.at[nxt], col_rs.at[slot], "rows", twin_r).start()

        arrived(fcol, col_rs, col_rs, "rows", k * per + (1 - side))
        rows = fcol[pl.ds(k * per, per)].reshape(block, width)
        keyed = dot(rows, wk[...])
        k_s[pl.ds(first, block), :] = keyed.astype(BF16)
        kt_s[k] = keyed.T.astype(BF16)
        valued = dot(rows, wv[...])
        v_s[pl.ds(first, block), :] = valued.astype(BF16)
        vt_s[k] = valued.T.astype(BF16)

        def pair(p, inner):
            lanes = pl.ds(pl.multiple_of(p * LANES, LANES), LANES)
            kp = k_s[pl.ds(first, block), lanes]
            m = mask_t[pl.ds(first, block), :]
            for a in range(2):
                h = 2 * p + a
                if keep:
                    e, raised, slope = terms(h, kp, v_s[pl.ds(first, block), lanes], m)
                    e_s[h, pl.ds(first, block), :] = e
                    a_s[h, pl.ds(first, block), :] = raised
                    b_s[h, pl.ds(first, block), :] = slope
                else:
                    e = weights_only(h, kp, m)
                vt = vt_s[k, pl.ds(pl.multiple_of(h * head, head), head), :]
                num_t[h] += dot(vt, e.astype(BF16))
                den_s[h] += jnp.sum(e.reshape(block // 8, 8, part), axis=0)
            return inner

        lax.fori_loop(0, HEADS // 2, pair, 0)
        return carry

    lax.fori_loop(0, chunks, forward, 0)

    for h in range(HEADS):
        low, high = (h % 2) * head, (h % 2 + 1) * head
        stat_send[0, h:h + 1] = jnp.sum(den_s[h], axis=0, keepdims=True)
        stat_send[1, h:h + 1] = jnp.sum(num_t[h] * ctm[h, low:high, :].astype(F32), axis=0, keepdims=True)
    for peer in col_peers:
        send(stat_send, stat_recv.at[me_c], st_ss.at[peer], st_rs.at[me_c], "cols", peer)
    stat_recv[me_c] = stat_send[...]
    for peer in col_peers:
        arrived(stat_recv, st_ss, st_rs, "cols", peer)
    total = jnp.sum(stat_recv[...], axis=0)
    inverse = 1.0 / total[0]
    inv_s[...] = inverse
    dl_s[...] = total[1] * inverse

    out_part = (num_t[...] * inverse[:, None, :]).reshape(width, part).T
    num_send[...] = out_part.astype(BF16).reshape(col_total, owned, width)
    for peer in col_peers:
        send(num_send.at[peer], num_recv.at[me_c], nu_ss.at[peer], nu_rs.at[me_c], "cols", peer)
    num_recv[me_c] = num_send[me_c]

    lane = lax.broadcasted_iota(jnp.int32, (part, LANES), 1)

    def pass_on(k):
        arrived(tw_recv, tw_rs, tw_rs, "rows", k)
        rg_send[k] = (rg_own[k] + tw_recv[k].astype(F32)).astype(BF16)
        remote(
            rg_send.at[k], rg_recv.at[me_k], rg_ss.at[k], rg_rs.at[me_k], "rows", k * per + side
        ).start()

    def backward(step, carry):
        k = flip(me_k, chunks - 1 - step, chunks)
        first = pl.multiple_of(k * block, block)

        def pair(p, inner):
            lanes = pl.ds(pl.multiple_of(p * LANES, LANES), LANES)
            qp = q_s[:, lanes]
            cp = crow[:, :, lanes].reshape(part, LANES)
            kg = jnp.zeros((block, LANES), F32)
            vg = jnp.zeros((block, LANES), F32)
            for a in range(2):
                h = 2 * p + a
                here = pl.ds(first, block)
                if keep:
                    e, raised, slope = e_s[h, here, :], a_s[h, here, :], b_s[h, here, :]
                else:
                    e, raised, slope = terms(h, k_s[here, lanes], v_s[here, lanes], mask_t[here, :])
                inv = inv_s[pl.ds(h, 1), :]
                gb = ((raised - slope * dl_s[pl.ds(h, 1), :]) * inv).astype(BF16)
                sb = (e * inv).astype(BF16)
                mine = (lane >= a * head) & (lane < (a + 1) * head)
                kt = kt_s[k, pl.ds(pl.multiple_of(h * head, head), head), :]
                qg_t[h] += dot(kt, gb)
                kg += dot(gb, jnp.where(mine, qp, jnp.zeros_like(qp)))
                vg += dot(sb, jnp.where(mine, cp, jnp.zeros_like(cp)))
            kg_s[:, lanes] = kg.astype(BF16)
            vg_s[:, lanes] = vg.astype(BF16)
            return inner

        lax.fori_loop(0, HEADS // 2, pair, 0)
        theirs, mine = pl.ds((1 - side) * owned, owned), pl.ds(side * owned, owned)
        sums = dot_t(kg_s[theirs, :], wk[...]) + dot_t(vg_s[theirs, :], wv[...])
        tw_send[k] = sums.astype(BF16)
        remote(tw_send.at[k], tw_recv.at[k], tw_ss.at[k], tw_rs.at[k], "rows", twin_r).start()
        rg_own[k] = dot_t(kg_s[mine, :], wk[...]) + dot_t(vg_s[mine, :], wv[...])

        @pl.when(step > 0)
        def _():
            pass_on(flip(me_k, chunks - step, chunks))

        return carry

    lax.fori_loop(0, chunks, backward, 0)

    query_grad = qg_t[...].reshape(width, part).T.astype(BF16)
    qg_send[...] = dot_t(query_grad, wq[...]).astype(BF16).reshape(col_total, owned, width)
    for peer in col_peers:
        send(qg_send.at[peer], qg_recv.at[me_c], qg_ss.at[peer], qg_rs.at[me_c], "cols", peer)
    qg_recv[me_c] = qg_send[me_c]

    for peer in col_peers:
        arrived(num_recv, nu_ss, nu_rs, "cols", peer)
    att_out[...] = jnp.sum(num_recv[...].astype(F32), axis=0).astype(BF16)
    arrived(tw_recv, tw_rs, tw_rs, "rows", me_k)
    grad = rg_own[me_k] + tw_recv[me_k].astype(F32)
    for x in line:
        arrived(rg_recv, rg_ss, rg_rs, "rows", x)
        grad += rg_recv[x].astype(F32)
    for peer in col_peers:
        arrived(qg_recv, qg_ss, qg_rs, "cols", peer)
    grad_out[...] = grad + jnp.sum(qg_recv[...].astype(F32), axis=0)

    for copy in sends:
        copy.wait_send()
    remote(tw_send.at[me_k], tw_recv.at[me_k], tw_ss.at[me_k], tw_rs.at[me_k], "rows", twin_r).wait_send()
    for x in line:
        slot = x * per + side
        remote(fcol.at[slot], fcol.at[slot], col_fs.at[x], col_rs.at[slot], "rows", twin_r).wait_send()
        remote(tw_send.at[x], tw_recv.at[x], tw_ss.at[x], tw_rs.at[x], "rows", twin_r).wait_send()
        remote(rg_send.at[x], rg_recv.at[me_k], rg_ss.at[x], rg_rs.at[me_k], "rows", slot).wait_send()


def local(row_total, col_total, features, w_query, w_key, w_value, cotangent, block_pairs, pair_count, edge_mask):
    owned, width = features.shape
    slots, block = edge_mask.shape[2], edge_mask.shape[3]
    part = owned * col_total
    span = owned * row_total
    chunks = span // block
    head = width // HEADS
    keep = span <= 512
    kept = (HEADS, span, part) if keep else (1, 8, LANES)
    vmem = pl.BlockSpec(memory_space=pltpu.VMEM)
    hbm = pl.BlockSpec(memory_space=pl.ANY)
    smem = pl.BlockSpec(memory_space=pltpu.SMEM)

    def buf(*shape, dtype=BF16):
        return pltpu.VMEM(shape, dtype)

    by_col = buf(col_total, owned, width)
    by_line = buf(chunks, owned, width)
    by_head = buf(HEADS, head, part, dtype=F32)
    kept_buf = buf(*kept, dtype=F32)
    square = buf(width, width)
    col_sem = pltpu.SemaphoreType.DMA((col_total,))
    row_sem = pltpu.SemaphoreType.DMA((row_total,))
    line_sem = pltpu.SemaphoreType.DMA((chunks,))
    scratch = [
        square, square, square, buf(slots, block, block, dtype=jnp.int32),
        buf(row_total, owned, width), by_col, by_col,
        buf(span, width), buf(span, width),
        buf(chunks, width, block), buf(chunks, width, block),
        buf(part, width), buf(HEADS, LANES, part), buf(HEADS, LANES, part),
        buf(span, part, dtype=F32), kept_buf, kept_buf, kept_buf,
        by_head, buf(HEADS, 8, part, dtype=F32),
        buf(HEADS, part, dtype=F32), buf(HEADS, part, dtype=F32),
        by_head, buf(block, width), buf(block, width),
        buf(2, HEADS, part, dtype=F32), buf(col_total, 2, HEADS, part, dtype=F32),
        by_col, by_col, by_col, by_col,
        by_line, by_line, buf(chunks, owned, width, dtype=F32), by_line, by_line,
        pltpu.SemaphoreType.DMA((7,)),
        line_sem, line_sem, row_sem,
        col_sem, col_sem, col_sem, col_sem, col_sem, col_sem, col_sem, col_sem,
        col_sem, col_sem, line_sem, line_sem, line_sem, line_sem,
    ]
    return pl.pallas_call(
        functools.partial(kernel, row_total, col_total, keep),
        out_shape=(
            jax.ShapeDtypeStruct((owned, width), BF16),
            jax.ShapeDtypeStruct((owned, width), F32),
        ),
        in_specs=[hbm, hbm, hbm, hbm, hbm, smem, smem, hbm],
        out_specs=(vmem, vmem),
        scratch_shapes=scratch,
        compiler_params=pltpu.CompilerParams(
            collective_id=0, has_side_effects=True, vmem_limit_bytes=56 * 1024 * 1024
        ),
    )(
        features, w_query, w_key, w_value, cotangent,
        block_pairs.reshape(slots, 2), pair_count, edge_mask.reshape(slots, block, block),
    )


def solution(mesh):
    in_specs = (
        P(("rows", "cols"), None),
        P(),
        P(),
        P(),
        P(("rows", "cols"), None),
        P("rows", "cols", None, None),
        P("rows", "cols"),
        P("rows", "cols", None, None, None),
    )
    out_specs = (P(("rows", "cols"), None), P(("rows", "cols"), None))
    body = functools.partial(local, mesh.shape["rows"], mesh.shape["cols"])
    return jax.shard_map(body, mesh=mesh, in_specs=in_specs, out_specs=out_specs, check_vma=False)
```

```python
import functools
import math

import jax
import jax.numpy as jnp
from jax import lax
from jax.experimental import pallas as pl
from jax.experimental.pallas import tpu as pltpu
from jax.sharding import PartitionSpec as P

HEADS = 8
SCORE_BOUND = 4.0
LANES = 128
MESH = pl.DeviceIdType.MESH
F32 = jnp.float32
BF16 = jnp.bfloat16


def dot(a, b):
    return jnp.dot(a, b, preferred_element_type=F32)


def kernel(
    row_total, col_total, keep,
    feat, wq_in, wk_in, wv_in, cot, pairs_in, count_in, mask_in,
    att_out, grad_out,
    pairs, count, wq, wk, wv, wqt, wkt, wvt, mask, fcol, frow, crow, k_s, v_s, kt_s, vt_s, q_s, qtm, ctm, mask_t, e_s, a_s, b_s,
    num_t, den_s, inv_s, dl_s, qg_t, kg_s, vg_s, g_s, s_s, sums_s, turn_s,
    stat_send, stat_recv, num_send, num_recv, qg_send, qg_recv,
    tw_send, tw_recv, rg_own, rg_send, rg_recv,
    load_s, col_ss, col_fs, col_rs, fr_ss, fr_rs, cr_ss, cr_rs, st_ss, st_rs, nu_ss, nu_rs,
    qg_ss, qg_rs, tw_ss, tw_rs, rg_ss, rg_rs,
):
    owned, width = feat.shape
    slots, block, _ = mask.shape
    head = width // HEADS
    part = owned * col_total
    row_blocks = part // block
    chunks = owned * row_total // block
    wide = math.gcd(chunks, 2)
    per = block // owned
    me_r = lax.axis_index("rows")
    me_c = lax.axis_index("cols")
    scale = 1.0 / (math.sqrt(head) * SCORE_BOUND)
    inverse_root = 1.0 / math.sqrt(head)

    def flip(index, amount, count_all):
        if count_all & (count_all - 1):
            return lax.rem(index + amount, count_all)
        out, bit = 0, 1
        while bit < count_all:
            out = out + bit * lax.rem(lax.div(index, bit) + lax.div(jnp.int32(amount), bit), 2)
            bit *= 2
        return out

    me_k, side = lax.div(me_r, per), lax.rem(me_r, per)
    twin_r = me_k * per + (1 - side)
    line = [flip(me_k, d, chunks) for d in range(1, chunks)]
    half, side_c = lax.div(me_c, 2), lax.rem(me_c, 2)
    twin_c = half * 2 + (1 - side_c)
    halves = [lax.rem(half + d, col_total // 2) for d in range(1, col_total // 2)]
    col_line = [x * 2 + side_c for x in halves]
    col_cross = [x * 2 + (1 - side_c) for x in halves]
    col_peers = col_cross + col_line + [twin_c]

    def remote(src, dst, ss, rs, axis, peer):
        return pltpu.make_async_remote_copy(
            src_ref=src, dst_ref=dst, send_sem=ss, recv_sem=rs,
            device_id={axis: peer}, device_id_type=MESH,
        )

    def arrived(buf, ss, rs, axis, src):
        remote(buf.at[src], buf.at[src], ss.at[src], rs.at[src], axis, src).wait_recv()

    loads = [
        pltpu.make_async_copy(src, dst, load_s.at[n])
        for n, (src, dst) in enumerate(
            [
                (mask_in, mask), (pairs_in, pairs), (count_in, count), (feat, frow.at[me_c]), (feat, fcol.at[me_r]), (cot, crow.at[me_c]),
                (wq_in, wq), (wk_in, wk), (wv_in, wv),
            ]
        )
    ]

    barrier = pltpu.get_barrier_semaphore()
    for peer in [twin_r] + [x * per + side for x in line]:
        pl.semaphore_signal(barrier, inc=1, device_id={"rows": peer}, device_id_type=MESH)
    for peer in col_peers:
        pl.semaphore_signal(barrier, inc=1, device_id={"cols": peer}, device_id_type=MESH)
    for load in loads:
        load.start()
    num_t[...] = jnp.zeros_like(num_t)
    den_s[...] = jnp.zeros_like(den_s)
    qg_t[...] = jnp.zeros_like(qg_t)
    for h in range(HEADS):
        other = (1 - h % 2) * head
        qtm[h, other:other + head, :] = jnp.zeros((head, part), BF16)
        ctm[h, other:other + head, :] = jnp.zeros((head, part), BF16)

    for load in loads[:3]:
        load.wait()
    live_total = count[0, 0]

    def mask_chunk(k, carry):
        for b in range(row_blocks):
            def find(s, found):
                hit = (pairs[0, 0, s, 0] == b) & (pairs[0, 0, s, 1] == k) & (s < live_total)
                return jnp.where(hit, s, found)

            found = lax.fori_loop(0, slots, find, jnp.int32(-1), unroll=slots <= 8)
            live = (found >= 0).astype(F32)
            tile = mask[jnp.maximum(found, 0)].astype(F32) * live
            j = lax.broadcasted_iota(jnp.int32, (block, block), 0) + k * block
            i = lax.broadcasted_iota(jnp.int32, (block, block), 1) + b * block
            own = i - me_c * owned
            same = (own == j - me_r * owned) & (own >= 0) & (own < owned)
            first = pl.multiple_of(k * block, block)
            mask_t[pl.ds(first, block), b * block:(b + 1) * block] = tile.T + same.astype(F32)
        return carry

    lax.fori_loop(0, chunks, mask_chunk, 0)

    pl.semaphore_wait(barrier, chunks + col_total - 1)

    sends = []

    def send(*args):
        copy = remote(*args)
        copy.start()
        sends.append(copy)

    for peer in col_line:
        send(feat, frow.at[me_c], fr_ss.at[peer], fr_rs.at[me_c], "cols", peer)
    send(feat, fcol.at[me_r], col_fs.at[me_k], col_rs.at[me_r], "rows", twin_r)
    for x in line:
        send(feat, fcol.at[me_r], col_ss.at[x], col_rs.at[me_r], "rows", x * per + side)
    send(feat, frow.at[me_c], fr_ss.at[me_c], fr_rs.at[me_c], "cols", twin_c)
    for peer in col_line:
        send(cot, crow.at[me_c], cr_ss.at[peer], cr_rs.at[me_c], "cols", peer)
    send(cot, crow.at[me_c], cr_ss.at[me_c], cr_rs.at[me_c], "cols", twin_c)

    def share_columns(buf, ss, rs):
        for peer in col_line:
            arrived(buf, ss, rs, "cols", peer)
            send(buf.at[peer], buf.at[peer], ss.at[peer + 1 - 2 * side_c], rs.at[peer], "cols", twin_c)
        for peer in [twin_c] + col_cross:
            arrived(buf, ss, rs, "cols", peer)

    for load in loads[3:]:
        load.wait()
    for straight, turned in ((wq, wqt), (wk, wkt), (wv, wvt)):
        turned[...] = straight[...].T
    def collect(k):
        arrived(fcol, col_rs, col_rs, "rows", k * per + (1 - side))

    def relay(k):
        slot = k * per + side
        arrived(fcol, col_rs, col_rs, "rows", slot)
        remote(fcol.at[slot], fcol.at[slot], col_fs.at[k], col_rs.at[slot], "rows", twin_r).start()

    tile = wide * block
    tiles = chunks // wide
    me_t = lax.div(me_k, wide)

    share_columns(frow, fr_ss, fr_rs)
    for w in range(1, wide):
        relay(me_t * wide + lax.rem(me_k - me_t * wide + w, wide))
    query = dot(frow[...].reshape(part, width), wq[...])
    q_s[...] = query.astype(BF16)
    query_t = query.T.astype(BF16)
    for h in range(HEADS):
        low, high = (h % 2) * head, (h % 2 + 1) * head
        qtm[h, low:high, :] = query_t[h * head:(h + 1) * head, :]
    share_columns(crow, cr_ss, cr_rs)
    grad_t = crow[...].reshape(part, width).astype(F32).T.astype(BF16)
    for h in range(HEADS):
        low, high = (h % 2) * head, (h % 2 + 1) * head
        ctm[h, low:high, :] = grad_t[h * head:(h + 1) * head, :]

    def terms(h, kp, vp, m):
        t = jnp.tanh(dot(kp, qtm[h]) * scale)
        e = m * jnp.exp(SCORE_BOUND * t)
        slope = e * ((1.0 - t * t) * inverse_root)
        return e, slope * dot(vp, ctm[h]), slope

    def weights_only(h, kp, m):
        return m * jnp.exp(SCORE_BOUND * jnp.tanh(dot(kp, qtm[h]) * scale))

    def forward(step, carry):
        g = flip(me_t, step, tiles)
        first = pl.multiple_of(g * tile, tile)
        here = pl.ds(first, tile)

        @pl.when(step + 1 < tiles)
        def _():
            nxt = flip(me_t, step + 1, tiles)
            for w in range(wide):
                relay(nxt * wide + w)

        for w in range(wide):
            collect(g * wide + w)
        rows = fcol[pl.ds(g * wide * per, wide * per)].reshape(tile, width)
        keyed = dot(rows, wk[...])
        k_s[here, :] = keyed.astype(BF16)
        keyed_t = keyed.T.astype(BF16)
        for w in range(wide):
            kt_s[g * wide + w] = keyed_t[:, w * block:(w + 1) * block]
        valued = dot(rows, wv[...])
        v_s[here, :] = valued.astype(BF16)
        vt_s[g] = valued.T.astype(BF16)

        def pair(p, inner):
            lanes = pl.ds(pl.multiple_of(p * LANES, LANES), LANES)
            kp = k_s[here, lanes]
            m = mask_t[here, :]
            for a in range(2):
                h = 2 * p + a
                if keep:
                    e, raised, slope = terms(h, kp, v_s[here, lanes], m)
                    e_s[h, here, :] = e
                    a_s[h, here, :] = raised
                    b_s[h, here, :] = slope
                else:
                    e = weights_only(h, kp, m)
                vt = vt_s[g, pl.ds(pl.multiple_of(h * head, head), head), :]
                num_t[h] += dot(vt, e.astype(BF16))
                den_s[h] += jnp.sum(e.reshape(tile // 8, 8, part), axis=0)
            return inner

        lax.fori_loop(0, HEADS // 2, pair, 0)
        return carry

    lax.fori_loop(0, tiles, forward, 0)

    for h in range(HEADS):
        low, high = (h % 2) * head, (h % 2 + 1) * head
        stat_send[0, h:h + 1] = jnp.sum(den_s[h], axis=0, keepdims=True)
        stat_send[1, h:h + 1] = jnp.sum(num_t[h] * ctm[h, low:high, :].astype(F32), axis=0, keepdims=True)
    for peer in col_peers:
        send(stat_send, stat_recv.at[me_c], st_ss.at[peer], st_rs.at[me_c], "cols", peer)
    stat_recv[me_c] = stat_send[...]
    num_part = num_t[...].reshape(width, part).T
    num_send[...] = num_part.astype(BF16).reshape(col_total, owned, width)
    for peer in col_peers:
        send(num_send.at[peer], num_recv.at[me_c], nu_ss.at[peer], nu_rs.at[me_c], "cols", peer)
    num_recv[me_c] = num_send[me_c]
    for peer in col_peers:
        arrived(stat_recv, st_ss, st_rs, "cols", peer)
    total = jnp.sum(stat_recv[...], axis=0)
    inverse = 1.0 / total[0]
    inv_s[...] = inverse
    dl_s[...] = total[1] * inverse

    lane = lax.broadcasted_iota(jnp.int32, (part, LANES), 1)

    def pass_on(k):
        arrived(tw_recv, tw_rs, tw_rs, "rows", k)
        rg_send[k] = (rg_own[k] + tw_recv[k].astype(F32)).astype(BF16)
        remote(
            rg_send.at[k], rg_recv.at[me_k], rg_ss.at[k], rg_rs.at[me_k], "rows", k * per + side
        ).start()

    def scores(k):
        here = pl.ds(pl.multiple_of(k * block, block), block)

        def pair(p, inner):
            lanes = pl.ds(pl.multiple_of(p * LANES, LANES), LANES)
            for a in range(2):
                h = 2 * p + a
                if keep:
                    e, raised, slope = e_s[h, here, :], a_s[h, here, :], b_s[h, here, :]
                else:
                    e, raised, slope = terms(h, k_s[here, lanes], v_s[here, lanes], mask_t[here, :])
                inv = inv_s[pl.ds(h, 1), :]
                gb = ((raised - slope * dl_s[pl.ds(h, 1), :]) * inv).astype(BF16)
                g_s[h] = gb
                s_s[h] = (e * inv).astype(BF16)
                kt = kt_s[k, pl.ds(pl.multiple_of(h * head, head), head), :]
                qg_t[h] += dot(kt, gb)
            return inner

        lax.fori_loop(0, HEADS // 2, pair, 0)

    def range_grads(k):
        def pair(p, inner):
            lanes = pl.ds(pl.multiple_of(p * LANES, LANES), LANES)
            qp = q_s[:, lanes]
            cp = crow[:, :, lanes].reshape(part, LANES)
            kg = jnp.zeros((block, LANES), F32)
            vg = jnp.zeros((block, LANES), F32)
            for a in range(2):
                h = 2 * p + a
                mine = (lane >= a * head) & (lane < (a + 1) * head)
                kg += dot(g_s[h], jnp.where(mine, qp, jnp.zeros_like(qp)))
                vg += dot(s_s[h], jnp.where(mine, cp, jnp.zeros_like(cp)))
            kg_s[:, lanes] = kg.astype(BF16)
            vg_s[:, lanes] = vg.astype(BF16)
            return inner

        lax.fori_loop(0, HEADS // 2, pair, 0)
        sums_s[...] = dot(kg_s[...], wkt[...]) + dot(vg_s[...], wvt[...])
        tw_send[k] = sums_s[pl.ds((1 - side) * owned, owned), :].astype(BF16)
        remote(tw_send.at[k], tw_recv.at[k], tw_ss.at[k], tw_rs.at[k], "rows", twin_r).start()
        rg_own[k] = sums_s[pl.ds(side * owned, owned), :]

    def backward(step, carry):
        k = flip(me_k, chunks - 1 - step, chunks)
        scores(k)
        range_grads(k)

        @pl.when(step > 0)
        def _():
            pass_on(flip(me_k, chunks - step, chunks))

        return carry

    lax.fori_loop(0, chunks - 1, backward, 0)
    scores(me_k)
    query_grad = qg_t[...].reshape(width, part).T.astype(BF16)
    qg_send[...] = dot(query_grad, wqt[...]).astype(BF16).reshape(col_total, owned, width)
    for peer in col_peers:
        send(qg_send.at[peer], qg_recv.at[me_c], qg_ss.at[peer], qg_rs.at[me_c], "cols", peer)
    qg_recv[me_c] = qg_send[me_c]
    if chunks > 1:
        pass_on(flip(me_k, 1, chunks))
    range_grads(me_k)

    turn_s[...] = jnp.broadcast_to(inv_s[...][:, None, :], (HEADS, head, part)).reshape(width, part).T
    for peer in col_peers:
        arrived(num_recv, nu_ss, nu_rs, "cols", peer)
    mine_inv = turn_s[pl.ds(pl.multiple_of(me_c * owned, owned), owned), :]
    att_out[...] = (jnp.sum(num_recv[...].astype(F32), axis=0) * mine_inv).astype(BF16)
    arrived(tw_recv, tw_rs, tw_rs, "rows", me_k)
    grad = rg_own[me_k] + tw_recv[me_k].astype(F32)
    for x in line:
        arrived(rg_recv, rg_ss, rg_rs, "rows", x)
        grad += rg_recv[x].astype(F32)
    for peer in col_peers:
        arrived(qg_recv, qg_ss, qg_rs, "cols", peer)
    grad_out[...] = grad + jnp.sum(qg_recv[...].astype(F32), axis=0)

    for copy in sends:
        copy.wait_send()
    remote(tw_send.at[me_k], tw_recv.at[me_k], tw_ss.at[me_k], tw_rs.at[me_k], "rows", twin_r).wait_send()
    for x in line:
        slot = x * per + side
        remote(fcol.at[slot], fcol.at[slot], col_fs.at[x], col_rs.at[slot], "rows", twin_r).wait_send()
        remote(tw_send.at[x], tw_recv.at[x], tw_ss.at[x], tw_rs.at[x], "rows", twin_r).wait_send()
        remote(rg_send.at[x], rg_recv.at[me_k], rg_ss.at[x], rg_rs.at[me_k], "rows", slot).wait_send()


def local(row_total, col_total, features, w_query, w_key, w_value, cotangent, block_pairs, pair_count, edge_mask):
    owned, width = features.shape
    slots, block = edge_mask.shape[2], edge_mask.shape[3]
    part = owned * col_total
    span = owned * row_total
    chunks = span // block
    head = width // HEADS
    wide = math.gcd(chunks, 2)
    keep = span <= 512
    kept = (HEADS, span, part) if keep else (1, 8, LANES)
    vmem = pl.BlockSpec(memory_space=pltpu.VMEM)
    hbm = pl.BlockSpec(memory_space=pl.ANY)

    def buf(*shape, dtype=BF16):
        return pltpu.VMEM(shape, dtype)

    by_col = buf(col_total, owned, width)
    by_line = buf(chunks, owned, width)
    by_head = buf(HEADS, head, part, dtype=F32)
    kept_buf = buf(*kept, dtype=F32)
    square = buf(width, width)
    col_sem = pltpu.SemaphoreType.DMA((col_total,))
    row_sem = pltpu.SemaphoreType.DMA((row_total,))
    line_sem = pltpu.SemaphoreType.DMA((chunks,))
    scratch = [
        pltpu.SMEM(block_pairs.shape, jnp.int32), pltpu.SMEM(pair_count.shape, jnp.int32),
        square, square, square, square, square, square, buf(slots, block, block, dtype=jnp.int32),
        buf(row_total, owned, width), by_col, by_col,
        buf(span, width), buf(span, width),
        buf(chunks, width, block), buf(chunks // wide, width, wide * block),
        buf(part, width), buf(HEADS, LANES, part), buf(HEADS, LANES, part),
        buf(span, part, dtype=F32), kept_buf, kept_buf, kept_buf,
        by_head, buf(HEADS, 8, part, dtype=F32),
        buf(HEADS, part, dtype=F32), buf(HEADS, part, dtype=F32),
        by_head, buf(block, width), buf(block, width),
        buf(HEADS, block, part), buf(HEADS, block, part),
        buf(block, width, dtype=F32), buf(part, width, dtype=F32),
        buf(2, HEADS, part, dtype=F32), buf(col_total, 2, HEADS, part, dtype=F32),
        by_col, by_col, by_col, by_col,
        by_line, by_line, buf(chunks, owned, width, dtype=F32), by_line, by_line,
        pltpu.SemaphoreType.DMA((9,)),
        line_sem, line_sem, row_sem,
        col_sem, col_sem, col_sem, col_sem, col_sem, col_sem, col_sem, col_sem,
        col_sem, col_sem, line_sem, line_sem, line_sem, line_sem,
    ]
    return pl.pallas_call(
        functools.partial(kernel, row_total, col_total, keep),
        out_shape=(
            jax.ShapeDtypeStruct((owned, width), BF16),
            jax.ShapeDtypeStruct((owned, width), F32),
        ),
        in_specs=[hbm] * 8,
        out_specs=(vmem, vmem),
        scratch_shapes=scratch,
        compiler_params=pltpu.CompilerParams(
            collective_id=0, has_side_effects=True, vmem_limit_bytes=56 * 1024 * 1024
        ),
    )(
        features, w_query, w_key, w_value, cotangent,
        block_pairs, pair_count, edge_mask.reshape(slots, block, block),
    )


def solution(mesh):
    in_specs = (
        P(("rows", "cols"), None),
        P(),
        P(),
        P(),
        P(("rows", "cols"), None),
        P("rows", "cols", None, None),
        P("rows", "cols"),
        P("rows", "cols", None, None, None),
    )
    out_specs = (P(("rows", "cols"), None), P(("rows", "cols"), None))
    body = functools.partial(local, mesh.shape["rows"], mesh.shape["cols"])
    return jax.shard_map(body, mesh=mesh, in_specs=in_specs, out_specs=out_specs, check_vma=False)
```

```python
import functools
import math

import jax
import jax.numpy as jnp
from jax import lax
from jax.experimental import pallas as pl
from jax.experimental.pallas import tpu as pltpu
from jax.sharding import PartitionSpec as P

HEADS = 8
SCORE_BOUND = 4.0
LANES = 128
MESH = pl.DeviceIdType.MESH
F32 = jnp.float32
BF16 = jnp.bfloat16


def dot(a, b):
    return jnp.dot(a, b, preferred_element_type=F32)


def kernel(
    row_total, col_total, keep,
    feat, wq_in, wk_in, wv_in, cot, pairs_in, count_in, mask_in,
    att_out, grad_out,
    pairs, count, wq, wk, wv, wqt, wkt, wvt, mask, fcol, frow, crow, k_s, v_s, kt_s, vt_s, q_s, qtm, ctm, mask_t, e_s, a_s, b_s,
    num_t, den_s, inv_s, dl_s, qg_t, kg_s, vg_s, g_s, s_s, sums_s, turn_s,
    stat_send, stat_recv, num_send, num_recv, qg_send, qg_recv,
    tw_send, tw_recv, rg_own, rg_send, rg_recv,
    load_s, col_ss, col_fs, col_rs, fr_ss, fr_rs, cr_ss, cr_rs, st_ss, st_rs, nu_ss, nu_rs,
    qg_ss, qg_rs, tw_ss, tw_rs, rg_ss, rg_rs,
):
    owned, width = feat.shape
    slots, block, _ = mask.shape
    head = width // HEADS
    part = owned * col_total
    row_blocks = part // block
    chunks = owned * row_total // block
    wide = math.gcd(chunks, 2)
    per = block // owned
    me_r = lax.axis_index("rows")
    me_c = lax.axis_index("cols")
    scale = 1.0 / (math.sqrt(head) * SCORE_BOUND)
    inverse_root = 1.0 / math.sqrt(head)

    def flip(index, amount, count_all):
        if count_all & (count_all - 1):
            return lax.rem(index + amount, count_all)
        out, bit = 0, 1
        while bit < count_all:
            out = out + bit * lax.rem(lax.div(index, bit) + lax.div(jnp.int32(amount), bit), 2)
            bit *= 2
        return out

    me_k, side = lax.div(me_r, per), lax.rem(me_r, per)
    twin_r = me_k * per + (1 - side)
    line = [flip(me_k, d, chunks) for d in range(1, chunks)]
    half, side_c = lax.div(me_c, 2), lax.rem(me_c, 2)
    twin_c = half * 2 + (1 - side_c)
    halves = [lax.rem(half + d, col_total // 2) for d in range(1, col_total // 2)]
    col_line = [x * 2 + side_c for x in halves]
    col_cross = [x * 2 + (1 - side_c) for x in halves]
    col_peers = col_cross + col_line + [twin_c]

    def remote(src, dst, ss, rs, axis, peer):
        return pltpu.make_async_remote_copy(
            src_ref=src, dst_ref=dst, send_sem=ss, recv_sem=rs,
            device_id={axis: peer}, device_id_type=MESH,
        )

    def arrived(buf, ss, rs, axis, src):
        remote(buf.at[src], buf.at[src], ss.at[src], rs.at[src], axis, src).wait_recv()

    loads = [
        pltpu.make_async_copy(src, dst, load_s.at[n])
        for n, (src, dst) in enumerate(
            [
                (mask_in, mask), (pairs_in, pairs), (count_in, count), (feat, frow.at[me_c]), (feat, fcol.at[me_r]), (cot, crow.at[me_c]),
                (wq_in, wq), (wk_in, wk), (wv_in, wv),
            ]
        )
    ]

    barrier = pltpu.get_barrier_semaphore()
    for peer in [twin_r] + [x * per + side for x in line]:
        pl.semaphore_signal(barrier, inc=1, device_id={"rows": peer}, device_id_type=MESH)
    for peer in col_peers:
        pl.semaphore_signal(barrier, inc=1, device_id={"cols": peer}, device_id_type=MESH)
    for load in loads:
        load.start()
    num_t[...] = jnp.zeros_like(num_t)
    den_s[...] = jnp.zeros_like(den_s)
    qg_t[...] = jnp.zeros_like(qg_t)
    for h in range(HEADS):
        other = (1 - h % 2) * head
        qtm[h, other:other + head, :] = jnp.zeros((head, part), BF16)
        ctm[h, other:other + head, :] = jnp.zeros((head, part), BF16)

    for load in loads[:3]:
        load.wait()
    live_total = count[0, 0]

    def mask_chunk(k, carry):
        for b in range(row_blocks):
            def find(s, found):
                hit = (pairs[0, 0, s, 0] == b) & (pairs[0, 0, s, 1] == k) & (s < live_total)
                return jnp.where(hit, s, found)

            found = lax.fori_loop(0, slots, find, jnp.int32(-1), unroll=slots <= 8)
            live = (found >= 0).astype(F32)
            tile = mask[jnp.maximum(found, 0)].astype(F32) * live
            j = lax.broadcasted_iota(jnp.int32, (block, block), 0) + k * block
            i = lax.broadcasted_iota(jnp.int32, (block, block), 1) + b * block
            own = i - me_c * owned
            same = (own == j - me_r * owned) & (own >= 0) & (own < owned)
            first = pl.multiple_of(k * block, block)
            mask_t[pl.ds(first, block), b * block:(b + 1) * block] = tile.T + same.astype(F32)
        return carry

    lax.fori_loop(0, chunks, mask_chunk, 0)

    pl.semaphore_wait(barrier, chunks + col_total - 1)

    sends = []

    def send(*args):
        copy = remote(*args)
        copy.start()
        sends.append(copy)

    for x in line:
        send(feat, fcol.at[me_r], col_ss.at[x], col_rs.at[me_r], "rows", x * per + side)
    for peer in col_line:
        send(feat, frow.at[me_c], fr_ss.at[peer], fr_rs.at[me_c], "cols", peer)
    send(feat, fcol.at[me_r], col_fs.at[me_k], col_rs.at[me_r], "rows", twin_r)
    send(feat, frow.at[me_c], fr_ss.at[me_c], fr_rs.at[me_c], "cols", twin_c)
    for peer in col_line:
        send(cot, crow.at[me_c], cr_ss.at[peer], cr_rs.at[me_c], "cols", peer)
    send(cot, crow.at[me_c], cr_ss.at[me_c], cr_rs.at[me_c], "cols", twin_c)

    def pass_columns(buf, ss, rs):
        for peer in col_line:
            arrived(buf, ss, rs, "cols", peer)
            send(buf.at[peer], buf.at[peer], ss.at[peer + 1 - 2 * side_c], rs.at[peer], "cols", twin_c)

    def take_columns(buf, ss, rs):
        for peer in [twin_c] + col_cross:
            arrived(buf, ss, rs, "cols", peer)

    for load in loads[3:]:
        load.wait()
    for straight, turned in ((wq, wqt), (wk, wkt), (wv, wvt)):
        turned[...] = straight[...].T
    def collect(k):
        arrived(fcol, col_rs, col_rs, "rows", k * per + (1 - side))

    def relay(k):
        slot = k * per + side
        arrived(fcol, col_rs, col_rs, "rows", slot)
        remote(fcol.at[slot], fcol.at[slot], col_fs.at[k], col_rs.at[slot], "rows", twin_r).start()

    tile = wide * block
    tiles = chunks // wide
    me_t = lax.div(me_k, wide)

    pass_columns(frow, fr_ss, fr_rs)
    pass_columns(crow, cr_ss, cr_rs)
    take_columns(frow, fr_ss, fr_rs)
    for w in range(1, wide):
        relay(me_t * wide + lax.rem(me_k - me_t * wide + w, wide))
    if tiles > 1:
        for w in range(wide):
            relay(flip(me_t, 1, tiles) * wide + w)
    query = dot(frow[...].reshape(part, width), wq[...])
    q_s[...] = query.astype(BF16)
    query_t = query.T.astype(BF16)
    for h in range(HEADS):
        low, high = (h % 2) * head, (h % 2 + 1) * head
        qtm[h, low:high, :] = query_t[h * head:(h + 1) * head, :]
    take_columns(crow, cr_ss, cr_rs)
    grad_t = crow[...].reshape(part, width).astype(F32).T.astype(BF16)
    for h in range(HEADS):
        low, high = (h % 2) * head, (h % 2 + 1) * head
        ctm[h, low:high, :] = grad_t[h * head:(h + 1) * head, :]

    def terms(h, kp, vp, m):
        t = jnp.tanh(dot(kp, qtm[h]) * scale)
        e = m * jnp.exp(SCORE_BOUND * t)
        slope = e * ((1.0 - t * t) * inverse_root)
        return e, slope * dot(vp, ctm[h]), slope

    def weights_only(h, kp, m):
        return m * jnp.exp(SCORE_BOUND * jnp.tanh(dot(kp, qtm[h]) * scale))

    def forward(step, carry):
        g = flip(me_t, step, tiles)
        first = pl.multiple_of(g * tile, tile)
        here = pl.ds(first, tile)

        @pl.when(step + 2 < tiles)
        def _():
            nxt = flip(me_t, step + 2, tiles)
            for w in range(wide):
                relay(nxt * wide + w)

        for w in range(wide):
            collect(g * wide + w)
        rows = fcol[pl.ds(g * wide * per, wide * per)].reshape(tile, width)
        keyed = dot(rows, wk[...])
        k_s[here, :] = keyed.astype(BF16)
        keyed_t = keyed.T.astype(BF16)
        for w in range(wide):
            kt_s[g * wide + w] = keyed_t[:, w * block:(w + 1) * block]
        valued = dot(rows, wv[...])
        v_s[here, :] = valued.astype(BF16)
        vt_s[g] = valued.T.astype(BF16)

        def pair(p, inner):
            lanes = pl.ds(pl.multiple_of(p * LANES, LANES), LANES)
            kp = k_s[here, lanes]
            m = mask_t[here, :]
            for a in range(2):
                h = 2 * p + a
                if keep:
                    e, raised, slope = terms(h, kp, v_s[here, lanes], m)
                    e_s[h, here, :] = e
                    a_s[h, here, :] = raised
                    b_s[h, here, :] = slope
                else:
                    e = weights_only(h, kp, m)
                vt = vt_s[g, pl.ds(pl.multiple_of(h * head, head), head), :]
                num_t[h] += dot(vt, e.astype(BF16))
                den_s[h] += jnp.sum(e.reshape(tile // 8, 8, part), axis=0)
            return inner

        lax.fori_loop(0, HEADS // 2, pair, 0)
        return carry

    lax.fori_loop(0, tiles, forward, 0)

    for h in range(HEADS):
        low, high = (h % 2) * head, (h % 2 + 1) * head
        stat_send[0, h:h + 1] = jnp.sum(den_s[h], axis=0, keepdims=True)
        stat_send[1, h:h + 1] = jnp.sum(num_t[h] * ctm[h, low:high, :].astype(F32), axis=0, keepdims=True)
    for peer in col_peers:
        send(stat_send, stat_recv.at[me_c], st_ss.at[peer], st_rs.at[me_c], "cols", peer)
    stat_recv[me_c] = stat_send[...]
    num_part = num_t[...].reshape(width, part).T
    num_send[...] = num_part.astype(BF16).reshape(col_total, owned, width)
    for peer in col_peers:
        send(num_send.at[peer], num_recv.at[me_c], nu_ss.at[peer], nu_rs.at[me_c], "cols", peer)
    num_recv[me_c] = num_send[me_c]
    for peer in col_peers:
        arrived(stat_recv, st_ss, st_rs, "cols", peer)
    total = jnp.sum(stat_recv[...], axis=0)
    inverse = 1.0 / total[0]
    inv_s[...] = inverse
    dl_s[...] = total[1] * inverse

    lane = lax.broadcasted_iota(jnp.int32, (part, LANES), 1)

    def pass_on(k):
        arrived(tw_recv, tw_rs, tw_rs, "rows", k)
        rg_send[k] = (rg_own[k] + tw_recv[k].astype(F32)).astype(BF16)
        remote(
            rg_send.at[k], rg_recv.at[me_k], rg_ss.at[k], rg_rs.at[me_k], "rows", k * per + side
        ).start()

    def scores(k):
        here = pl.ds(pl.multiple_of(k * block, block), block)

        def pair(p, inner):
            lanes = pl.ds(pl.multiple_of(p * LANES, LANES), LANES)
            for a in range(2):
                h = 2 * p + a
                if keep:
                    e, raised, slope = e_s[h, here, :], a_s[h, here, :], b_s[h, here, :]
                else:
                    e, raised, slope = terms(h, k_s[here, lanes], v_s[here, lanes], mask_t[here, :])
                inv = inv_s[pl.ds(h, 1), :]
                gb = ((raised - slope * dl_s[pl.ds(h, 1), :]) * inv).astype(BF16)
                g_s[h] = gb
                s_s[h] = (e * inv).astype(BF16)
                kt = kt_s[k, pl.ds(pl.multiple_of(h * head, head), head), :]
                qg_t[h] += dot(kt, gb)
            return inner

        lax.fori_loop(0, HEADS // 2, pair, 0)

    def range_grads(k):
        def pair(p, inner):
            lanes = pl.ds(pl.multiple_of(p * LANES, LANES), LANES)
            qp = q_s[:, lanes]
            cp = crow[:, :, lanes].reshape(part, LANES)
            kg = jnp.zeros((block, LANES), F32)
            vg = jnp.zeros((block, LANES), F32)
            for a in range(2):
                h = 2 * p + a
                mine = (lane >= a * head) & (lane < (a + 1) * head)
                kg += dot(g_s[h], jnp.where(mine, qp, jnp.zeros_like(qp)))
                vg += dot(s_s[h], jnp.where(mine, cp, jnp.zeros_like(cp)))
            kg_s[:, lanes] = kg.astype(BF16)
            vg_s[:, lanes] = vg.astype(BF16)
            return inner

        lax.fori_loop(0, HEADS // 2, pair, 0)
        sums_s[...] = dot(kg_s[...], wkt[...]) + dot(vg_s[...], wvt[...])
        tw_send[k] = sums_s[pl.ds((1 - side) * owned, owned), :].astype(BF16)
        remote(tw_send.at[k], tw_recv.at[k], tw_ss.at[k], tw_rs.at[k], "rows", twin_r).start()
        rg_own[k] = sums_s[pl.ds(side * owned, owned), :]

    def backward(step, carry):
        k = flip(me_k, chunks - 1 - step, chunks)
        scores(k)
        range_grads(k)

        @pl.when(step > 0)
        def _():
            pass_on(flip(me_k, chunks - step, chunks))

        return carry

    lax.fori_loop(0, chunks - 1, backward, 0)
    scores(me_k)
    query_grad = qg_t[...].reshape(width, part).T.astype(BF16)
    qg_send[...] = dot(query_grad, wqt[...]).astype(BF16).reshape(col_total, owned, width)
    for peer in col_peers:
        send(qg_send.at[peer], qg_recv.at[me_c], qg_ss.at[peer], qg_rs.at[me_c], "cols", peer)
    qg_recv[me_c] = qg_send[me_c]
    if chunks > 1:
        pass_on(flip(me_k, 1, chunks))
    range_grads(me_k)

    turn_s[...] = jnp.broadcast_to(inv_s[...][:, None, :], (HEADS, head, part)).reshape(width, part).T
    for peer in col_peers:
        arrived(num_recv, nu_ss, nu_rs, "cols", peer)
    mine_inv = turn_s[pl.ds(pl.multiple_of(me_c * owned, owned), owned), :]
    att_out[...] = (jnp.sum(num_recv[...].astype(F32), axis=0) * mine_inv).astype(BF16)
    arrived(tw_recv, tw_rs, tw_rs, "rows", me_k)
    grad = rg_own[me_k] + tw_recv[me_k].astype(F32)
    for x in line:
        arrived(rg_recv, rg_ss, rg_rs, "rows", x)
        grad += rg_recv[x].astype(F32)
    for peer in col_peers:
        arrived(qg_recv, qg_ss, qg_rs, "cols", peer)
    grad_out[...] = grad + jnp.sum(qg_recv[...].astype(F32), axis=0)

    for copy in sends:
        copy.wait_send()
    remote(tw_send.at[me_k], tw_recv.at[me_k], tw_ss.at[me_k], tw_rs.at[me_k], "rows", twin_r).wait_send()
    for x in line:
        slot = x * per + side
        remote(fcol.at[slot], fcol.at[slot], col_fs.at[x], col_rs.at[slot], "rows", twin_r).wait_send()
        remote(tw_send.at[x], tw_recv.at[x], tw_ss.at[x], tw_rs.at[x], "rows", twin_r).wait_send()
        remote(rg_send.at[x], rg_recv.at[me_k], rg_ss.at[x], rg_rs.at[me_k], "rows", slot).wait_send()


def local(row_total, col_total, features, w_query, w_key, w_value, cotangent, block_pairs, pair_count, edge_mask):
    owned, width = features.shape
    slots, block = edge_mask.shape[2], edge_mask.shape[3]
    part = owned * col_total
    span = owned * row_total
    chunks = span // block
    head = width // HEADS
    wide = math.gcd(chunks, 2)
    keep = span <= 512
    kept = (HEADS, span, part) if keep else (1, 8, LANES)
    vmem = pl.BlockSpec(memory_space=pltpu.VMEM)
    hbm = pl.BlockSpec(memory_space=pl.ANY)

    def buf(*shape, dtype=BF16):
        return pltpu.VMEM(shape, dtype)

    by_col = buf(col_total, owned, width)
    by_line = buf(chunks, owned, width)
    by_head = buf(HEADS, head, part, dtype=F32)
    kept_buf = buf(*kept, dtype=F32)
    square = buf(width, width)
    col_sem = pltpu.SemaphoreType.DMA((col_total,))
    row_sem = pltpu.SemaphoreType.DMA((row_total,))
    line_sem = pltpu.SemaphoreType.DMA((chunks,))
    scratch = [
        pltpu.SMEM(block_pairs.shape, jnp.int32), pltpu.SMEM(pair_count.shape, jnp.int32),
        square, square, square, square, square, square, buf(slots, block, block, dtype=jnp.int32),
        buf(row_total, owned, width), by_col, by_col,
        buf(span, width), buf(span, width),
        buf(chunks, width, block), buf(chunks // wide, width, wide * block),
        buf(part, width), buf(HEADS, LANES, part), buf(HEADS, LANES, part),
        buf(span, part, dtype=F32), kept_buf, kept_buf, kept_buf,
        by_head, buf(HEADS, 8, part, dtype=F32),
        buf(HEADS, part, dtype=F32), buf(HEADS, part, dtype=F32),
        by_head, buf(block, width), buf(block, width),
        buf(HEADS, block, part), buf(HEADS, block, part),
        buf(block, width, dtype=F32), buf(part, width, dtype=F32),
        buf(2, HEADS, part, dtype=F32), buf(col_total, 2, HEADS, part, dtype=F32),
        by_col, by_col, by_col, by_col,
        by_line, by_line, buf(chunks, owned, width, dtype=F32), by_line, by_line,
        pltpu.SemaphoreType.DMA((9,)),
        line_sem, line_sem, row_sem,
        col_sem, col_sem, col_sem, col_sem, col_sem, col_sem, col_sem, col_sem,
        col_sem, col_sem, line_sem, line_sem, line_sem, line_sem,
    ]
    return pl.pallas_call(
        functools.partial(kernel, row_total, col_total, keep),
        out_shape=(
            jax.ShapeDtypeStruct((owned, width), BF16),
            jax.ShapeDtypeStruct((owned, width), F32),
        ),
        in_specs=[hbm] * 8,
        out_specs=(vmem, vmem),
        scratch_shapes=scratch,
        compiler_params=pltpu.CompilerParams(
            collective_id=0, has_side_effects=True, vmem_limit_bytes=56 * 1024 * 1024
        ),
    )(
        features, w_query, w_key, w_value, cotangent,
        block_pairs, pair_count, edge_mask.reshape(slots, block, block),
    )


def solution(mesh):
    in_specs = (
        P(("rows", "cols"), None),
        P(),
        P(),
        P(),
        P(("rows", "cols"), None),
        P("rows", "cols", None, None),
        P("rows", "cols"),
        P("rows", "cols", None, None, None),
    )
    out_specs = (P(("rows", "cols"), None), P(("rows", "cols"), None))
    body = functools.partial(local, mesh.shape["rows"], mesh.shape["cols"])
    return jax.shard_map(body, mesh=mesh, in_specs=in_specs, out_specs=out_specs, check_vma=False)
```
